32 devices in a mesh: gx: 16 (over z, y, core), gy: 2 (over x).
Axes of the slice: x: 2, y: 2, z: 4, core: 2. Of those that a mesh axis runs over, the one named last changes fastest.
Arguments:
- displacement: float32 [3, 128, 16, 128], P(None, 'gx', 'gy'), may hold values from -0.6 to 0.6
- velocity: float32 [3, 128, 16, 128], P(None, 'gx', 'gy'), may hold values from -0.6 to 0.6
- cuts: int32 [16, 128, 16, 128], P(None, 'gx', 'gy'), may hold values from 0 to 3
- material: int32 [128, 16, 128], P('gx', 'gy'), may hold values from 0 to 7
- micromodulus: float32 [8], replicated, may hold values from 0.2 to 2
- cot_disp: float32 [3, 128, 16, 128], P(None, 'gx', 'gy'), may hold values from -6 to 6
- cot_vel: float32 [3, 128, 16, 128], P(None, 'gx', 'gy'), may hold values from -6 to 6
Outputs:
- grad_disp: float32 [3, 128, 16, 128], P(None, 'gx', 'gy')
- grad_vel: float32 [3, 128, 16, 128], P(None, 'gx', 'gy')
- grad_micro: float32 [8], replicated
The draws below stay inside these ranges and needn't reach their ends.
All inputs are finite; a program needn't handle non-finite values.
Results may differ from the reference program's by a relative error of at most 0.0001.
Values sent between devices are 32-bit elements; how exact they have to be, the bound alone decides.
A program may use at most 128 MiB of HBM per device.

```python
import math
import jax
import jax.numpy as jnp
from jax import lax

NZ = 128
STEPS = 4
NCLASS = 8
NX = 128
NY = 16


def plant(array, stream_key, low, largest):
    longest = array.shape.index(max(array.shape))
    spots = []
    for shift in (0, 1):
        where = [jax.random.randint(jax.random.fold_in(stream_key, axis), (), 0, length) for axis, length in enumerate(array.shape)]
        where[longest] = (where[longest] + shift) % array.shape[longest]
        spots.append(tuple(where))
    return array.at[spots[0]].set(low).at[spots[1]].set(largest)


def shard_levels(rng, shape, shards, least, high):
    def one(axis_at, parts):
        steps = jax.random.uniform(jax.random.fold_in(jax.random.fold_in(rng, 6), axis_at), (parts,), jnp.float32, least / len(shards), high / len(shards))
        return jnp.repeat(jnp.exp(steps), shape[axis_at] // parts).reshape((-1,) + (1,) * (len(shape) - axis_at - 1))

    factor_of = one(*shards[0])
    for cut in shards[1:]:
        factor_of = factor_of * one(*cut)
    return factor_of


def noise(own_key, dims, width, reach, shards=(), kind=jnp.bfloat16):
    gain = shard_levels(own_key, dims, shards, -0.22, 0.18) if shards else 1.0
    values = jax.random.normal(own_key, dims, jnp.float32) * width * gain
    return jnp.minimum(jnp.maximum(values, -reach), reach).astype(kind)


def setup_inputs(seed: int = 0) -> dict:
    seeds = jax.random.split(jax.random.key(seed), 8)
    return {
        "displacement": noise(seeds[0], (3, NX, NY, NZ), 0.1, 0.6, ((1, 16), (2, 2)), jnp.float32),
        "velocity": noise(seeds[1], (3, NX, NY, NZ), 0.1, 0.6, ((1, 16), (2, 2)), jnp.float32),
        "cuts": plant(jax.random.randint(seeds[2], (16, NX, NY, NZ), 0, 4), jax.random.fold_in(seeds[2], 1), 0, 3).astype(jnp.int32),
        "material": plant(jax.random.randint(seeds[3], (NX, NY, NZ), 0, NCLASS), jax.random.fold_in(seeds[3], 1), 0, NCLASS - 1).astype(jnp.int32),
        "micromodulus": jnp.clip(jnp.exp(jax.random.uniform(seeds[4], (NCLASS,), jnp.float32, math.log(0.2), math.log(2.0))), 0.2, 2.0),
        "cot_disp": noise(seeds[5], (3, NX, NY, NZ), 1.0, 6.0, ((1, 16), (2, 2)), jnp.float32),
        "cot_vel": noise(seeds[6], (3, NX, NY, NZ), 1.0, 6.0, ((1, 16), (2, 2)), jnp.float32),
    }


BOND_OFFSETS = ((1, 0, 0), (0, 1, 0), (0, 0, 1), (1, 1, 0), (1, -1, 0), (1, 0, 1), (1, 0, -1), (0, 1, 1), (0, 1, -1), (2, 0, 0), (0, 2, 0), (0, 0, 2), (1, 1, 1), (1, -1, 1), (1, 1, -1), (1, -1, -1))
TIME_STEP = 0.2

def bond_keep(cuts, start_x, start_y, total_x, total_y):
    grid_shape = cuts.shape[1:]
    pos_x = lax.broadcasted_iota(jnp.int32, grid_shape, 0) + start_x
    pos_y = lax.broadcasted_iota(jnp.int32, grid_shape, 1) + start_y
    pos_z = lax.broadcasted_iota(jnp.int32, grid_shape, 2)
    total_z = grid_shape[2]
    layers = []
    for bond_id, offset in enumerate(BOND_OFFSETS):
        inside = (pos_x + offset[0] >= 0) & (pos_x + offset[0] < total_x)
        inside = inside & (pos_y + offset[1] >= 0) & (pos_y + offset[1] < total_y)
        inside = inside & (pos_z + offset[2] >= 0) & (pos_z + offset[2] < total_z)
        weakened = 1.0 / (1.0 + cuts[bond_id].astype(jnp.float32))
        layers.append(jnp.where(inside, weakened, jnp.zeros_like(weakened)))
    return jnp.stack(layers)

def class_lookup(table, material):
    result = jnp.zeros(material.shape, table.dtype)
    for class_id in range(table.shape[0]):
        result = jnp.where(material == class_id, table[class_id], result)
    return result

def class_sums(weight, material, count_classes):
    return jnp.stack([jnp.sum(jnp.where(material == class_id, weight, jnp.zeros_like(weight))) for class_id in range(count_classes)])

def window(source, anchor, extent):
    return source[..., anchor[0]:anchor[0] + extent[0], anchor[1]:anchor[1] + extent[1], anchor[2]:anchor[2] + extent[2]]

def stretched(owner_u, partner_u, offset):
    length_sq = float(offset[0] * offset[0] + offset[1] * offset[1] + offset[2] * offset[2])
    w_x = offset[0] + partner_u[0] - owner_u[0]
    w_y = offset[1] + partner_u[1] - owner_u[1]
    w_z = offset[2] + partner_u[2] - owner_u[2]
    stretch = (w_x * w_x + w_y * w_y + w_z * w_z - length_sq) / (2.0 * length_sq)
    return (jnp.stack([w_x, w_y, w_z]), stretch, length_sq)

def bond_frame(offset, inner_size):
    lower = tuple((min(2, 2 - offset[d]) for d in range(3)))
    extent = tuple((inner_size[d] + abs(offset[d]) for d in range(3)))
    target = tuple((lower[d] + offset[d] for d in range(3)))
    at_owner = tuple((2 - lower[d] for d in range(3)))
    at_back = tuple((2 - offset[d] - lower[d] for d in range(3)))
    return (lower, extent, target, at_owner, at_back)

def net_force(padded, stiff_pad):
    inner_size = tuple((padded.shape[d] - 4 for d in range(1, 4)))
    total_force = jnp.zeros((3,) + inner_size, padded.dtype)
    for bond_id, offset in enumerate(BOND_OFFSETS):
        length = math.sqrt(offset[0] ** 2 + offset[1] ** 2 + offset[2] ** 2)
        lower, extent, target, at_owner, at_back = bond_frame(offset, inner_size)
        stretch_vec, stretch, length_sq = stretched(window(padded, lower, extent), window(padded, target, extent), offset)
        stiffness = window(stiff_pad[bond_id], lower, extent)
        bond_push = stiffness * stretch / length * stretch_vec
        total_force = total_force + window(bond_push, at_owner, inner_size) - window(bond_push, at_back, inner_size)
    return total_force

def force_adjoint(padded, cot_pad, stiff_pad, keep_frac):
    inner_size = tuple((padded.shape[d] - 4 for d in range(1, 4)))
    pulled = jnp.zeros((3,) + inner_size, padded.dtype)
    class_part = jnp.zeros(inner_size, padded.dtype)
    for bond_id, offset in enumerate(BOND_OFFSETS):
        length = math.sqrt(offset[0] ** 2 + offset[1] ** 2 + offset[2] ** 2)
        lower, extent, target, at_owner, at_back = bond_frame(offset, inner_size)
        stretch_vec, stretch, length_sq = stretched(window(padded, lower, extent), window(padded, target, extent), offset)
        force_cot = window(cot_pad, lower, extent) - window(cot_pad, target, extent)
        inner_dot = lax.optimization_barrier(jnp.sum(stretch_vec * force_cot, axis=0))
        stiffness = window(stiff_pad[bond_id], lower, extent)
        bond_pull = stiffness * stretch / length * force_cot + stiffness * inner_dot / (length * length_sq) * stretch_vec
        pulled = pulled + window(bond_pull, at_back, inner_size) - window(bond_pull, at_owner, inner_size)
        class_part = class_part + keep_frac[bond_id] * window(stretch * inner_dot, at_owner, inner_size) / length
    return (pulled, class_part)

def pad_all(values):
    return jnp.pad(values, ((0, 0), (2, 2), (2, 2), (2, 2)))

def reference(displacement, velocity, cuts, material, micromodulus, cot_disp, cot_vel):
    grid_size = displacement.shape[1:]
    keep_frac = bond_keep(cuts, 0, 0, grid_size[0], grid_size[1])
    node_mu = class_lookup(micromodulus, material)
    stiff_pad = pad_all(node_mu[None] * keep_frac)
    states = []
    disp_now, vel_now = (displacement, velocity)
    for step_no in range(STEPS):
        states.append(disp_now)
        if step_no + 1 < STEPS:
            net_push = net_force(pad_all(disp_now), stiff_pad)
            vel_now = vel_now + TIME_STEP * net_push
            disp_now = disp_now + TIME_STEP * vel_now
    disp_cot, vel_cot = (cot_disp, cot_vel)
    class_weight = jnp.zeros(grid_size, jnp.float32)
    for step_no in reversed(range(STEPS)):
        vel_total = vel_cot + TIME_STEP * disp_cot
        pulled, class_part = force_adjoint(pad_all(states[step_no]), pad_all(vel_total), stiff_pad, keep_frac)
        disp_cot = disp_cot + TIME_STEP * pulled
        vel_cot = vel_total
        class_weight = class_weight + TIME_STEP * class_part
    total_nodes = grid_size[0] * grid_size[1] * grid_size[2]
    micro_grad = class_sums(class_weight, material, NCLASS) / math.sqrt(total_nodes)
    return (disp_cot, vel_cot, micro_grad)
```

```python
import math

import jax
import jax.numpy as jnp
from jax import lax
from jax.experimental import pallas as pl
from jax.experimental.pallas import tpu as pltpu
from jax.sharding import PartitionSpec as P

STEPS = 4
NCLASS = 8
TIME_STEP = 0.2
MESH = pl.DeviceIdType.MESH

BONDS = (
    (0, 0, 1),
    (0, 0, 2),
    (0, 1, 0),
    (0, 1, 1),
    (0, 1, -1),
    (0, 2, 0),
    (1, 1, 0),
    (1, 1, 1),
    (1, 1, -1),
    (1, 0, 0),
    (1, 0, 1),
    (1, 0, -1),
    (1, -1, 0),
    (1, -1, 1),
    (1, -1, -1),
    (2, 0, 0),
)
REF_BONDS = (
    (1, 0, 0),
    (0, 1, 0),
    (0, 0, 1),
    (1, 1, 0),
    (1, -1, 0),
    (1, 0, 1),
    (1, 0, -1),
    (0, 1, 1),
    (0, 1, -1),
    (2, 0, 0),
    (0, 2, 0),
    (0, 0, 2),
    (1, 1, 1),
    (1, -1, 1),
    (1, 1, -1),
    (1, -1, -1),
)
CUT_ROW = tuple(REF_BONDS.index(o) for o in BONDS)
UP_Y = range(2, 9)
DOWN_Y = range(12, 15)
DIRS = ((1, 0), (-1, 0), (0, 1), (0, -1), (1, 1), (1, -1), (-1, 1), (-1, -1))
Y0 = 8


def make_kernel(nx, ny, bx, by, nz):
    assert by == 8 and nz == 128
    nf = 2 * STEPS
    inv_nodes = 1.0 / math.sqrt(nx * bx * ny * by * nz)

    def kernel(
        disp, vel, cuts, material, micro, cot_d, cot_v,
        out_a, out_g, out_m,
        fld, rolled_u, rolled_g, stiff, back, vnow, anow, msum,
        pack_y, land_y, pack_c, land_c,
        kpack_u, kland_u, kpack_d, kland_d, kpack_c, kland_c,
        part_x, part_y, mine,
        ssem, rsem, kssem, krsem, psem, qsem,
    ):
        ix = lax.axis_index("gx")
        iy = lax.axis_index("gy")

        def there(sx, sy):
            ok = None
            for pos, step, count in ((ix, sx, nx), (iy, sy, ny)):
                if step:
                    one = (pos + step >= 0) & (pos + step < count)
                    ok = one if ok is None else ok & one
            return ok

        def who(sx, sy):
            return (ix + sx, iy + sy)

        barrier = pltpu.get_barrier_semaphore()
        for j in range(1, nx):
            pl.semaphore_signal(barrier, inc=1, device_id=(lax.rem(ix + j, nx), iy), device_id_type=MESH)
        for j in range(1, ny):
            pl.semaphore_signal(barrier, inc=1, device_id=(ix, lax.rem(iy + j, ny)), device_id_type=MESH)
        for sx, sy in DIRS:
            if sx and sy:
                @pl.when(there(sx, sy))
                def _():
                    pl.semaphore_signal(barrier, inc=1, device_id=who(sx, sy), device_id_type=MESH)

        def copies(f, d):
            sx, sy = DIRS[d]
            if sy == 0:
                a, b = (bx, 0) if sx > 0 else (2, bx + 2)
                src = fld.at[f, :, pl.ds(a, 2), pl.ds(Y0, 8), :]
                dst = fld.at[f, :, pl.ds(b, 2), pl.ds(Y0, 8), :]
            elif sx == 0:
                e = 0 if sy > 0 else 1
                src, dst = pack_y.at[f, e], land_y.at[f, e]
            else:
                src, dst = pack_c.at[f, d - 4], land_c.at[f, d - 4]
            return pltpu.make_async_remote_copy(
                src_ref=src, dst_ref=dst, send_sem=ssem.at[f, d], recv_sem=rsem.at[f, d],
                device_id=who(sx, sy), device_id_type=MESH,
            )

        def send_field(f):
            for d in (0, 1):
                @pl.when(there(*DIRS[d]))
                def _():
                    copies(f, d).start()
            for d in (4, 5, 6, 7):
                sx, sy = DIRS[d]
                x0 = bx if sx > 0 else 2
                y0 = Y0 + 6 if sy > 0 else Y0
                @pl.when(there(sx, sy))
                def _():
                    for c in range(3):
                        for i in range(2):
                            pack_c[f, d - 4, pl.ds(c * 4 + i * 2, 2), :] = fld[f, c, x0 + i, pl.ds(y0, 2), :]
                    copies(f, d).start()
            for d in (2, 3):
                sx, sy = DIRS[d]
                y0 = Y0 + 6 if sy > 0 else Y0
                @pl.when(there(sx, sy))
                def _():
                    for c in range(3):
                        for i in range(bx):
                            pack_y[f, d - 2, pl.ds((c * bx + i) * 2, 2), :] = fld[f, c, 2 + i, pl.ds(y0, 2), :]
                    copies(f, d).start()

        def recv_field(f):
            for d in range(8):
                sx, sy = DIRS[d]
                y0 = Y0 - 2 if sy > 0 else Y0 + 8
                @pl.when(there(-sx, -sy))
                def _():
                    copies(f, d).wait_recv()
                    for c in range(3):
                        if sx == 0:
                            for i in range(bx):
                                fld[f, c, 2 + i, pl.ds(y0, 2), :] = land_y[f, d - 2, pl.ds((c * bx + i) * 2, 2), :]
                        elif sy:
                            x0 = 0 if sx > 0 else bx + 2
                            for i in range(2):
                                fld[f, c, x0 + i, pl.ds(y0, 2), :] = land_c[f, d - 4, pl.ds(c * 4 + i * 2, 2), :]

        for c in range(3):
            for x in range(bx):
                fld[0, c, 2 + x, pl.ds(Y0, 8), :] = disp[c, x]
                vnow[c, x] = vel[c, x]
                anow[c, x] = cot_d[c, x]
                fld[2 * STEPS - 1, c, 2 + x, pl.ds(Y0, 8), :] = cot_v[c, x] + TIME_STEP * cot_d[c, x]

        zero = jnp.zeros((8, nz), jnp.float32)
        zero24 = jnp.zeros((24, nz), jnp.float32)

        count = nx - 1 + ny - 1
        diag = jnp.int32(0)
        for sx, sy in DIRS:
            if sx and sy:
                diag = diag + jnp.where(there(sx, sy), 1, 0).astype(jnp.int32)
        pl.semaphore_wait(barrier, diag + count)

        send_field(0)

        py = lax.broadcasted_iota(jnp.int32, (8, nz), 0) + iy * by
        pz = lax.broadcasted_iota(jnp.int32, (8, nz), 1)

        def own_stiff(x, carry):
            mat = material[x]
            mu = jnp.zeros((8, nz), jnp.float32)
            for cl in range(NCLASS):
                mu = jnp.where(mat == cl, micro[cl], mu)
            px = jnp.full((8, nz), ix * bx + x, jnp.int32)
            for k, (dx, dy, dz) in enumerate(BONDS):
                ok = None
                for pos, step, total in ((px, dx, nx * bx), (py, dy, ny * by), (pz, dz, nz)):
                    if step:
                        one = pos < total - step if step > 0 else pos >= -step
                        ok = one if ok is None else ok & one
                n2 = dx * dx + dy * dy + dz * dz
                scaled = mu * (0.5 / (n2 * math.sqrt(n2)))
                keep = scaled / (1.0 + cuts[CUT_ROW[k], x].astype(jnp.float32))
                stiff[k, 2 + x, pl.ds(Y0, 8), :] = jnp.where(ok, keep, 0.0)
            return carry

        lax.fori_loop(0, bx, own_stiff, 0)

        def kcopies():
            return (
                (1, 0, stiff.at[pl.ds(6, 9), bx + 1, pl.ds(Y0, 8), :], stiff.at[pl.ds(6, 9), 1, pl.ds(Y0, 8), :]),
                (1, 0, stiff.at[15, pl.ds(bx, 2), pl.ds(Y0, 8), :], stiff.at[15, pl.ds(0, 2), pl.ds(Y0, 8), :]),
                (1, 1, kpack_c.at[0], kland_c.at[0]),
                (1, -1, kpack_c.at[1], kland_c.at[1]),
                (0, -1, kpack_d, kland_d),
                (0, 1, kpack_u, kland_u),
            )

        def kcopy(j):
            sx, sy, src, dst = kcopies()[j]
            return pltpu.make_async_remote_copy(
                src_ref=src, dst_ref=dst, send_sem=kssem.at[j], recv_sem=krsem.at[j],
                device_id=who(sx, sy), device_id_type=MESH,
            )

        KDIRS = ((1, 0), (1, 0), (1, 1), (1, -1), (0, -1), (0, 1))
        for j, (sx, sy) in enumerate(KDIRS):
            @pl.when(there(sx, sy))
            def _():
                row = Y0 + 7 if sy > 0 else Y0
                if j == 2 or j == 3:
                    for n, k in enumerate((6, 7, 8) if j == 2 else (12, 13, 14)):
                        kpack_c[j - 2, pl.ds(n, 1), :] = stiff[k, bx + 1, pl.ds(row, 1), :]
                if j == 4:
                    for n, k in enumerate(DOWN_Y):
                        for x in range(bx):
                            kpack_d[pl.ds(n * bx + x, 1), :] = stiff[k, 2 + x, pl.ds(row, 1), :]
                if j == 5:
                    for n, k in enumerate(UP_Y):
                        for x in range(bx):
                            kpack_u[pl.ds(n * bx + x, 1), :] = stiff[k, 2 + x, pl.ds(row, 1), :]
                    for x in range(bx):
                        kpack_u[pl.ds(7 * bx + x, 1), :] = stiff[5, 2 + x, pl.ds(row - 1, 1), :]
                kcopy(j).start()

        send_field(2 * STEPS - 1)

        for cond, planes in ((ix == 0, (0, 1)), (ix == nx - 1, (bx + 2, bx + 3))):
            @pl.when(cond)
            def _():
                for f in range(nf):
                    for c in range(3):
                        for x in planes:
                            fld[f, c, x] = zero24
                if planes[0] == 0:
                    for k in range(6, 16):
                        for x in planes:
                            stiff[k, x] = zero24
        for cond, row in ((iy == 0, 0), (iy == ny - 1, 16)):
            @pl.when(cond)
            def _():
                def clear(x, carry):
                    for f in range(nf):
                        for c in range(3):
                            fld[f, c, x, pl.ds(row, 8), :] = zero
                    for k in UP_Y if row == 0 else DOWN_Y:
                        stiff[k, x, pl.ds(row, 8), :] = zero
                    return carry
                lax.fori_loop(0, bx + 4, clear, 0)

        recv_field(0)

        for j, (sx, sy) in enumerate(KDIRS):
            @pl.when(there(-sx, -sy))
            def _():
                kcopy(j).wait_recv()
                row = Y0 - 1 if sy > 0 else Y0 + 8
                if j == 2 or j == 3:
                    for n, k in enumerate((6, 7, 8) if j == 2 else (12, 13, 14)):
                        stiff[k, 1, pl.ds(row, 1), :] = kland_c[j - 2, pl.ds(n, 1), :]
                if j == 4:
                    for n, k in enumerate(DOWN_Y):
                        for x in range(bx):
                            stiff[k, 2 + x, pl.ds(row, 1), :] = kland_d[pl.ds(n * bx + x, 1), :]
                if j == 5:
                    for n, k in enumerate(UP_Y):
                        for x in range(bx):
                            stiff[k, 2 + x, pl.ds(row, 1), :] = kland_u[pl.ds(n * bx + x, 1), :]
                    for x in range(bx):
                        stiff[5, 2 + x, pl.ds(row - 1, 1), :] = kland_u[pl.ds(7 * bx + x, 1), :]

        def back_stiff(x, carry):
            for k, (dx, dy, dz) in enumerate(BONDS):
                val = stiff[k, 2 + x - dx, pl.ds(Y0 - dy, 8), :]
                if dz:
                    val = pltpu.roll(val, dz % nz, 1)
                back[k, x] = val
            return carry

        lax.fori_loop(0, bx, back_stiff, 0)

        def roll_field(f, out):
            def one(x, carry):
                for c in range(3):
                    for r in (Y0 - 1, Y0 + 1):
                        val = fld[f, c, x, pl.ds(r, 8), :]
                        out[0, c, x, pl.ds(r, 8), :] = pltpu.roll(val, nz - 1, 1)
                        out[1, c, x, pl.ds(r, 8), :] = pltpu.roll(val, 1, 1)
                return carry
            lax.fori_loop(1, bx + 3, one, 0)

        def get(f, out, c, x, off, centre):
            dx, dy, dz = off
            if abs(dz) == 2:
                return pltpu.roll(centre, (-dz) % nz, 1)
            if dz:
                return out[0 if dz > 0 else 1, c, x + 2 + dx, pl.ds(Y0 + dy, 8), :]
            return fld[f, c, x + 2 + dx, pl.ds(Y0 + dy, 8), :]

        def bond_list():
            for k, o in enumerate(BONDS):
                yield k, False, o
                yield k, True, tuple(-e for e in o)

        def coef(k, rev, x):
            return back[k, x] if rev else stiff[k, x + 2, pl.ds(Y0, 8), :]

        def vectors(f, x, off, cent, shifted):
            return [get(f, rolled_u, c, x, off, cent[c]) - shifted[c][off[c]] for c in range(3)]

        def centres(f, x):
            cent = [fld[f, c, x + 2, pl.ds(Y0, 8), :] for c in range(3)]
            shifted = [{e: cent[c] - float(e) for e in (-2, -1, 0, 1, 2)} for c in range(3)]
            return cent, shifted

        def forward(n):
            roll_field(n, rolled_u)

            def one(x, carry):
                cent, shifted = centres(n, x)
                acc = [jnp.zeros((8, nz), jnp.float32)] * 3
                for k, rev, off in bond_list():
                    w = vectors(n, x, off, cent, shifted)
                    n2 = float(sum(e * e for e in off))
                    s = (w[0] * w[0] + w[1] * w[1] + w[2] * w[2]) - n2
                    t = coef(k, rev, x) * s
                    acc = [acc[c] + t * w[c] for c in range(3)]
                for c in range(3):
                    v = vnow[c, x] + TIME_STEP * acc[c]
                    vnow[c, x] = v
                    fld[n + 1, c, x + 2, pl.ds(Y0, 8), :] = cent[c] + TIME_STEP * v
                return carry

            lax.fori_loop(0, bx, one, 0)

        def adjoint(n):
            gf = STEPS + n
            roll_field(gf, rolled_g)
            roll_field(n, rolled_u)

            def one(x, carry):
                cent, shifted = centres(n, x)
                gc = [fld[gf, c, x + 2, pl.ds(Y0, 8), :] for c in range(3)]
                acc = [jnp.zeros((8, nz), jnp.float32)] * 3
                bcc = [jnp.zeros((8, nz), jnp.float32)] * 3
                m = jnp.zeros((8, nz), jnp.float32)
                for k, rev, off in bond_list():
                    w = vectors(n, x, off, cent, shifted)
                    g = [gc[c] - get(gf, rolled_g, c, x, off, gc[c]) for c in range(3)]
                    n2 = float(sum(e * e for e in off))
                    s = (w[0] * w[0] + w[1] * w[1] + w[2] * w[2]) - n2
                    dot = w[0] * g[0] + w[1] * g[1] + w[2] * g[2]
                    kk = coef(k, rev, x)
                    t = kk * s
                    r = kk * dot
                    if not rev:
                        m = m + s * r
                    acc = [acc[c] + t * g[c] for c in range(3)]
                    bcc = [bcc[c] + r * w[c] for c in range(3)]
                for c in range(3):
                    a = anow[c, x] - TIME_STEP * (acc[c] + 2.0 * bcc[c])
                    if n:
                        anow[c, x] = a
                        fld[gf - 1, c, x + 2, pl.ds(Y0, 8), :] = gc[c] + TIME_STEP * a
                    else:
                        out_a[c, x] = a
                        out_g[c, x] = gc[c]
                msum[x] = m if n == STEPS - 1 else msum[x] + m
                return carry

            lax.fori_loop(0, bx, one, 0)

        for n in range(STEPS - 1):
            forward(n)
            send_field(n + 1)
            recv_field(n + 1)
        recv_field(2 * STEPS - 1)
        for n in reversed(range(STEPS)):
            adjoint(n)
            if n:
                send_field(STEPS + n - 1)
                recv_field(STEPS + n - 1)

        lane = lax.broadcasted_iota(jnp.int32, (1, nz), 1)
        row = jnp.zeros((1, nz), jnp.float32)
        for cl in range(NCLASS):
            tot = jnp.zeros((8, nz), jnp.float32)
            for x in range(bx):
                tot = tot + jnp.where(material[x] == cl, msum[x], 0.0)
            one = jnp.sum(jnp.sum(tot, axis=0, keepdims=True), axis=1, keepdims=True)
            row = jnp.where(lane == cl, one * (TIME_STEP * inv_nodes) / micro[cl], row)
        mine[0] = row

        def spread(src, land, axis_pos, size, ident, sems):
            outs = []
            for j in range(1, size):
                cp = pltpu.make_async_remote_copy(
                    src_ref=src, dst_ref=land.at[j - 1], send_sem=sems.at[0, j - 1], recv_sem=sems.at[1, j - 1],
                    device_id=ident(lax.rem(axis_pos + j, size)), device_id_type=MESH,
                )
                cp.start()
                outs.append(cp)
            return outs

        outs = spread(mine.at[0], part_x, ix, nx, lambda j: (j, iy), psem)
        for cp in outs:
            cp.wait_recv()
        tot = mine[0]
        for j in range(nx - 1):
            tot = tot + part_x[j]
        mine[1] = tot
        outs_y = spread(mine.at[1], part_y, iy, ny, lambda j: (ix, j), qsem)
        for cp in outs_y:
            cp.wait_recv()
        for j in range(ny - 1):
            tot = tot + part_y[j]
        out_m[...] = tot

        for cp in outs + outs_y:
            cp.wait_send()
        for f in range(nf):
            for d in range(8):
                @pl.when(there(*DIRS[d]))
                def _():
                    copies(f, d).wait_send()
        for j, (sx, sy) in enumerate(KDIRS):
            @pl.when(there(sx, sy))
            def _():
                kcopy(j).wait_send()

    return kernel


def solution(mesh):
    nx, ny = mesh.shape["gx"], mesh.shape["gy"]

    def body(displacement, velocity, cuts, material, micromodulus, cot_disp, cot_vel):
        bx, by, nz = material.shape
        nf = 2 * STEPS
        f32 = jnp.float32
        vmem = pl.BlockSpec(memory_space=pltpu.VMEM)
        smem = pl.BlockSpec(memory_space=pltpu.SMEM)
        grad_a, grad_g, micro = pl.pallas_call(
            make_kernel(nx, ny, bx, by, nz),
            out_shape=(
                jax.ShapeDtypeStruct((3, bx, by, nz), f32),
                jax.ShapeDtypeStruct((3, bx, by, nz), f32),
                jax.ShapeDtypeStruct((1, nz), f32),
            ),
            in_specs=[vmem] * 4 + [smem] + [vmem] * 2,
            out_specs=(vmem, vmem, vmem),
            scratch_shapes=[
                pltpu.VMEM((nf, 3, bx + 4, 24, nz), f32),
                pltpu.VMEM((2, 3, bx + 4, 24, nz), f32),
                pltpu.VMEM((2, 3, bx + 4, 24, nz), f32),
                pltpu.VMEM((16, bx + 4, 24, nz), f32),
                pltpu.VMEM((16, bx, 8, nz), f32),
                pltpu.VMEM((3, bx, 8, nz), f32),
                pltpu.VMEM((3, bx, 8, nz), f32),
                pltpu.VMEM((bx, 8, nz), f32),
                pltpu.VMEM((nf, 2, 6 * bx, nz), f32),
                pltpu.VMEM((nf, 2, 6 * bx, nz), f32),
                pltpu.VMEM((nf, 4, 16, nz), f32),
                pltpu.VMEM((nf, 4, 16, nz), f32),
                pltpu.VMEM((8 * bx, nz), f32),
                pltpu.VMEM((8 * bx, nz), f32),
                pltpu.VMEM((3 * bx, nz), f32),
                pltpu.VMEM((3 * bx, nz), f32),
                pltpu.VMEM((2, 8, nz), f32),
                pltpu.VMEM((2, 8, nz), f32),
                pltpu.VMEM((nx, 1, nz), f32),
                pltpu.VMEM((ny, 1, nz), f32),
                pltpu.VMEM((2, 1, nz), f32),
                pltpu.SemaphoreType.DMA((nf, 8)),
                pltpu.SemaphoreType.DMA((nf, 8)),
                pltpu.SemaphoreType.DMA((6,)),
                pltpu.SemaphoreType.DMA((6,)),
                pltpu.SemaphoreType.DMA((2, nx)),
                pltpu.SemaphoreType.DMA((2, ny)),
            ],
            compiler_params=pltpu.CompilerParams(
                collective_id=0, has_side_effects=True, vmem_limit_bytes=40 * 1024 * 1024
            ),
        )(displacement, velocity, cuts, material, micromodulus, cot_disp, cot_vel)
        return grad_a, grad_g, micro[0, :NCLASS]

    return jax.shard_map(
        body,
        mesh=mesh,
        in_specs=(
            P(None, "gx", "gy", None),
            P(None, "gx", "gy", None),
            P(None, "gx", "gy", None),
            P("gx", "gy", None),
            P(),
            P(None, "gx", "gy", None),
            P(None, "gx", "gy", None),
        ),
        out_specs=(P(None, "gx", "gy", None), P(None, "gx", "gy", None), P()),
        check_vma=False,
    )
```

```python
import math

import jax
import jax.numpy as jnp
from jax import lax
from jax.experimental import pallas as pl
from jax.experimental.pallas import tpu as pltpu
from jax.sharding import PartitionSpec as P

STEPS = 4
NCLASS = 8
TIME_STEP = 0.2
MESH = pl.DeviceIdType.MESH

BONDS = (
    (0, 0, 1),
    (0, 0, 2),
    (0, 1, 0),
    (0, 1, 1),
    (0, 1, -1),
    (0, 2, 0),
    (1, 1, 0),
    (1, 1, 1),
    (1, 1, -1),
    (1, 0, 0),
    (1, 0, 1),
    (1, 0, -1),
    (1, -1, 0),
    (1, -1, 1),
    (1, -1, -1),
    (2, 0, 0),
)
REF_BONDS = (
    (1, 0, 0),
    (0, 1, 0),
    (0, 0, 1),
    (1, 1, 0),
    (1, -1, 0),
    (1, 0, 1),
    (1, 0, -1),
    (0, 1, 1),
    (0, 1, -1),
    (2, 0, 0),
    (0, 2, 0),
    (0, 0, 2),
    (1, 1, 1),
    (1, -1, 1),
    (1, 1, -1),
    (1, -1, -1),
)
CUT_ROW = tuple(REF_BONDS.index(o) for o in BONDS)
UP_Y = range(2, 9)
DOWN_Y = range(12, 15)
DIRS = ((1, 0), (-1, 0), (0, 1), (0, -1), (1, 1), (1, -1), (-1, 1), (-1, -1))
Y0 = 8


def make_kernel(nx, ny, bx, by, nz):
    assert by == 8 and nz == 128
    nf = 2 * STEPS
    inv_nodes = 1.0 / math.sqrt(nx * bx * ny * by * nz)

    def kernel(
        disp, vel, cuts_in, material_in, micro, cot_d, cot_v,
        out_a, out_g, out_m,
        fld, rolled, cuts, material, cot_in, tval, stiff, back, vnow, anow, msum,
        pack_y, land_y, roll_y, pack_c, land_c,
        kpack_u, kland_u, kpack_d, kland_d, kpack_c, kland_c,
        part, mine,
        isem, ssem, rsem, kssem, krsem, psem, qsem,
    ):
        ix = lax.axis_index("gx")
        iy = lax.axis_index("gy")

        def there(sx, sy):
            ok = None
            for pos, step, count in ((ix, sx, nx), (iy, sy, ny)):
                if step:
                    one = (pos + step >= 0) & (pos + step < count)
                    ok = one if ok is None else ok & one
            return ok

        def who(sx, sy):
            return (ix + sx, iy + sy)

        barrier = pltpu.get_barrier_semaphore()
        me = ix * ny + iy

        def peer(j):
            to = lax.rem(me + j, nx * ny)
            return (to // ny, lax.rem(to, ny))

        def greet(j, carry):
            pl.semaphore_signal(barrier, inc=1, device_id=peer(j), device_id_type=MESH)
            return carry

        lax.fori_loop(1, nx * ny, greet, 0)

        loads = [
            pltpu.make_async_copy(src, dst, isem.at[j])
            for j, (src, dst) in enumerate((
                (cuts_in, cuts),
                (material_in, material),
                (disp, fld.at[0, :, pl.ds(2, bx), pl.ds(Y0, 8), :]),
                (cot_v, cot_in),
                (cot_d, anow),
                (vel, vnow),
            ))
        ]
        for cp in loads:
            cp.start()

        def copies(f, d):
            sx, sy = DIRS[d]
            if sy == 0:
                a, b = (bx, 0) if sx > 0 else (2, bx + 2)
                src = fld.at[f, :, pl.ds(a, 2), pl.ds(Y0, 8), :]
                dst = fld.at[f, :, pl.ds(b, 2), pl.ds(Y0, 8), :]
            elif sx == 0:
                e = 0 if sy > 0 else 1
                src, dst = pack_y.at[f, e], land_y.at[f, e]
            else:
                src, dst = pack_c.at[f, d - 4], land_c.at[f, d - 4]
            return pltpu.make_async_remote_copy(
                src_ref=src, dst_ref=dst, send_sem=ssem.at[f, d], recv_sem=rsem.at[f, d],
                device_id=who(sx, sy), device_id_type=MESH,
            )

        def send_field(f):
            for d in (0, 1):
                @pl.when(there(*DIRS[d]))
                def _():
                    copies(f, d).start()
            for d in (4, 5, 6, 7):
                sx, sy = DIRS[d]
                x0 = bx if sx > 0 else 2
                y0 = Y0 + 6 if sy > 0 else Y0
                @pl.when(there(sx, sy))
                def _():
                    for c in range(3):
                        for i in range(2):
                            pack_c[f, d - 4, pl.ds(c * 4 + i * 2, 2), :] = fld[f, c, x0 + i, pl.ds(y0, 2), :]
                    copies(f, d).start()
            for d in (2, 3):
                sx, sy = DIRS[d]
                y0 = Y0 + 6 if sy > 0 else Y0
                @pl.when(there(sx, sy))
                def _():
                    for c in range(3):
                        for i in range(bx):
                            pack_y[f, d - 2, pl.ds((c * bx + i) * 2, 2), :] = fld[f, c, 2 + i, pl.ds(y0, 2), :]
                    copies(f, d).start()

        def turn(val, dz):
            return pltpu.roll(val, (-dz) % nz, 1)

        def roll_own(f):
            def some(i, carry):
                for c in range(3):
                    for x in range(4):
                        val = fld[f, c, 2 + i * 4 + x, pl.ds(Y0, 8), :]
                        rolled[f, 0, c, 2 + i * 4 + x, pl.ds(Y0, 8), :] = turn(val, 1)
                        rolled[f, 1, c, 2 + i * 4 + x, pl.ds(Y0, 8), :] = turn(val, -1)
                return carry
            lax.fori_loop(0, bx // 4, some, 0)

        def recv_field(f):
            for d in range(8):
                sx, sy = DIRS[d]
                y0 = Y0 - 2 if sy > 0 else Y0 + 8
                near = Y0 - 1 if sy > 0 else Y0 + 8
                j0 = 1 if sy > 0 else 0
                @pl.when(there(-sx, -sy))
                def _():
                    copies(f, d).wait_recv()
                    if sy == 0:
                        x = 1 if sx > 0 else bx + 2
                        for c in range(3):
                            val = fld[f, c, x, pl.ds(Y0, 8), :]
                            rolled[f, 0, c, x, pl.ds(Y0, 8), :] = turn(val, 1)
                            rolled[f, 1, c, x, pl.ds(Y0, 8), :] = turn(val, -1)
                    elif sx == 0:
                        for i in range(6 * bx // 8):
                            val = land_y[f, d - 2, pl.ds(i * 8, 8), :]
                            roll_y[0, pl.ds(i * 8, 8), :] = turn(val, 1)
                            roll_y[1, pl.ds(i * 8, 8), :] = turn(val, -1)
                        for c in range(3):
                            for i in range(bx):
                                r = (c * bx + i) * 2
                                fld[f, c, 2 + i, pl.ds(y0, 2), :] = land_y[f, d - 2, pl.ds(r, 2), :]
                                for z in range(2):
                                    rolled[f, z, c, 2 + i, pl.ds(near, 1), :] = roll_y[z, pl.ds(r + j0, 1), :]
                    else:
                        x = 1 if sx > 0 else bx + 2
                        i = 1 if sx > 0 else 0
                        for h in range(2):
                            val = land_c[f, d - 4, pl.ds(h * 8, 8), :]
                            roll_y[0, pl.ds(h * 8, 8), :] = turn(val, 1)
                            roll_y[1, pl.ds(h * 8, 8), :] = turn(val, -1)
                        for c in range(3):
                            r = c * 4 + i * 2 + j0
                            fld[f, c, x, pl.ds(near, 1), :] = land_c[f, d - 4, pl.ds(r, 1), :]
                            for z in range(2):
                                rolled[f, z, c, x, pl.ds(near, 1), :] = roll_y[z, pl.ds(r, 1), :]

        zero = jnp.zeros((8, nz), jnp.float32)
        zero24 = jnp.zeros((24, nz), jnp.float32)

        py = lax.broadcasted_iota(jnp.int32, (8, nz), 0) + iy * by
        pz = lax.broadcasted_iota(jnp.int32, (8, nz), 1)

        def own_stiff(x, carry):
            mat = material[x]
            mu = jnp.zeros((8, nz), jnp.float32)
            for cl in range(NCLASS):
                mu = jnp.where(mat == cl, micro[cl], mu)
            px = jnp.full((8, nz), ix * bx + x, jnp.int32)
            for k, (dx, dy, dz) in enumerate(BONDS):
                ok = None
                for pos, step, total in ((px, dx, nx * bx), (py, dy, ny * by), (pz, dz, nz)):
                    if step:
                        one = pos < total - step if step > 0 else pos >= -step
                        ok = one if ok is None else ok & one
                n2 = dx * dx + dy * dy + dz * dz
                scaled = mu * (0.5 / (n2 * math.sqrt(n2)))
                keep = scaled / (1.0 + cuts[CUT_ROW[k], x].astype(jnp.float32))
                stiff[k, 2 + x, pl.ds(Y0, 8), :] = jnp.where(ok, keep, 0.0)
            return carry

        loads[0].wait()
        loads[1].wait()
        lax.fori_loop(0, bx, own_stiff, 0)

        for cp in loads[2:]:
            cp.wait()
        for c in range(3):
            for x in range(bx):
                fld[2 * STEPS - 1, c, 2 + x, pl.ds(Y0, 8), :] = cot_in[c, x] + TIME_STEP * anow[c, x]

        pl.semaphore_wait(barrier, nx * ny - 1)
        send_field(0)

        def kcopies():
            return (
                (1, 0, stiff.at[pl.ds(6, 9), bx + 1, pl.ds(Y0, 8), :], stiff.at[pl.ds(6, 9), 1, pl.ds(Y0, 8), :]),
                (1, 0, stiff.at[15, pl.ds(bx, 2), pl.ds(Y0, 8), :], stiff.at[15, pl.ds(0, 2), pl.ds(Y0, 8), :]),
                (1, 1, kpack_c.at[0], kland_c.at[0]),
                (1, -1, kpack_c.at[1], kland_c.at[1]),
                (0, -1, kpack_d, kland_d),
                (0, 1, kpack_u, kland_u),
            )

        def kcopy(j):
            sx, sy, src, dst = kcopies()[j]
            return pltpu.make_async_remote_copy(
                src_ref=src, dst_ref=dst, send_sem=kssem.at[j], recv_sem=krsem.at[j],
                device_id=who(sx, sy), device_id_type=MESH,
            )

        KDIRS = ((1, 0), (1, 0), (1, 1), (1, -1), (0, -1), (0, 1))
        for j, (sx, sy) in enumerate(KDIRS):
            @pl.when(there(sx, sy))
            def _():
                row = Y0 + 7 if sy > 0 else Y0
                if j == 2 or j == 3:
                    for n, k in enumerate((6, 7, 8) if j == 2 else (12, 13, 14)):
                        kpack_c[j - 2, pl.ds(n, 1), :] = stiff[k, bx + 1, pl.ds(row, 1), :]
                if j == 4:
                    for n, k in enumerate(DOWN_Y):
                        for x in range(bx):
                            kpack_d[pl.ds(n * bx + x, 1), :] = stiff[k, 2 + x, pl.ds(row, 1), :]
                if j == 5:
                    for n, k in enumerate(UP_Y):
                        for x in range(bx):
                            kpack_u[pl.ds(n * bx + x, 1), :] = stiff[k, 2 + x, pl.ds(row, 1), :]
                    for x in range(bx):
                        kpack_u[pl.ds(7 * bx + x, 1), :] = stiff[5, 2 + x, pl.ds(row - 1, 1), :]
                kcopy(j).start()

        send_field(2 * STEPS - 1)
        roll_own(0)
        roll_own(2 * STEPS - 1)

        for cond, planes in ((ix == 0, (0, 1)), (ix == nx - 1, (bx + 2, bx + 3))):
            @pl.when(cond)
            def _():
                for f in range(nf):
                    for c in range(3):
                        for x in planes:
                            fld[f, c, x] = zero24
                        rolled[f, 0, c, planes[0] if planes[0] else 1] = zero24
                        rolled[f, 1, c, planes[0] if planes[0] else 1] = zero24
                if planes[0] == 0:
                    for k in range(6, 16):
                        for x in planes:
                            stiff[k, x] = zero24
        for cond, row in ((iy == 0, 0), (iy == ny - 1, 16)):
            @pl.when(cond)
            def _():
                def clear(x, carry):
                    for f in range(nf):
                        for c in range(3):
                            fld[f, c, x, pl.ds(row, 8), :] = zero
                            rolled[f, 0, c, x, pl.ds(row, 8), :] = zero
                            rolled[f, 1, c, x, pl.ds(row, 8), :] = zero
                    for k in UP_Y if row == 0 else DOWN_Y:
                        stiff[k, x, pl.ds(row, 8), :] = zero
                    return carry
                lax.fori_loop(0, bx + 4, clear, 0)

        recv_field(0)

        for j, (sx, sy) in enumerate(KDIRS):
            @pl.when(there(-sx, -sy))
            def _():
                kcopy(j).wait_recv()
                row = Y0 - 1 if sy > 0 else Y0 + 8
                if j == 2 or j == 3:
                    for n, k in enumerate((6, 7, 8) if j == 2 else (12, 13, 14)):
                        stiff[k, 1, pl.ds(row, 1), :] = kland_c[j - 2, pl.ds(n, 1), :]
                if j == 4:
                    for n, k in enumerate(DOWN_Y):
                        for x in range(bx):
                            stiff[k, 2 + x, pl.ds(row, 1), :] = kland_d[pl.ds(n * bx + x, 1), :]
                if j == 5:
                    for n, k in enumerate(UP_Y):
                        for x in range(bx):
                            stiff[k, 2 + x, pl.ds(row, 1), :] = kland_u[pl.ds(n * bx + x, 1), :]
                    for x in range(bx):
                        stiff[5, 2 + x, pl.ds(row - 1, 1), :] = kland_u[pl.ds(7 * bx + x, 1), :]

        def back_stiff(x, carry):
            for k, (dx, dy, dz) in enumerate(BONDS):
                val = stiff[k, 2 + x - dx, pl.ds(Y0 - dy, 8), :]
                if dz:
                    val = pltpu.roll(val, dz % nz, 1)
                back[k, x] = val
            return carry

        lax.fori_loop(0, bx, back_stiff, 0)

        def get(f, c, x, off, centre):
            dx, dy, dz = off
            if abs(dz) == 2:
                return turn(centre, dz)
            if dz:
                return rolled[f, 0 if dz > 0 else 1, c, x + 2 + dx, pl.ds(Y0 + dy, 8), :]
            return fld[f, c, x + 2 + dx, pl.ds(Y0 + dy, 8), :]

        def bond_list():
            for k, o in enumerate(BONDS):
                yield k, False, o
                yield k, True, tuple(-e for e in o)

        def coef(k, rev, x):
            return back[k, x] if rev else stiff[k, x + 2, pl.ds(Y0, 8), :]

        def vectors(f, x, off, cent, shifted):
            return [get(f, c, x, off, cent[c]) - shifted[c][off[c]] for c in range(3)]

        def centres(f, x):
            cent = [fld[f, c, x + 2, pl.ds(Y0, 8), :] for c in range(3)]
            shifted = [{e: cent[c] - float(e) for e in (-2, -1, 0, 1, 2)} for c in range(3)]
            return cent, shifted

        def stretch(w, off):
            return (w[0] * w[0] + w[1] * w[1] + w[2] * w[2]) - float(sum(e * e for e in off))

        def forward(n):
            def one(x, carry):
                cent, shifted = centres(n, x)
                acc = [jnp.zeros((8, nz), jnp.float32)] * 3
                for k, rev, off in bond_list():
                    w = vectors(n, x, off, cent, shifted)
                    t = coef(k, rev, x) * stretch(w, off)
                    tval[n, 2 * k + rev, x] = t
                    acc = [acc[c] + t * w[c] for c in range(3)]
                for c in range(3):
                    v = vnow[c, x] + TIME_STEP * acc[c]
                    vnow[c, x] = v
                    fld[n + 1, c, x + 2, pl.ds(Y0, 8), :] = cent[c] + TIME_STEP * v
                return carry

            lax.fori_loop(0, bx, one, 0)

        def micro_part():
            def one(x, carry):
                cent, shifted = centres(0, x)
                gc = [fld[STEPS, c, x + 2, pl.ds(Y0, 8), :] for c in range(3)]
                m = msum[x]
                for k, rev, off in bond_list():
                    if rev:
                        continue
                    w = vectors(0, x, off, cent, shifted)
                    g = [gc[c] - get(STEPS, c, x, off, gc[c]) for c in range(3)]
                    m = m + tval[0, 2 * k, x] * (w[0] * g[0] + w[1] * g[1] + w[2] * g[2])
                msum[x] = m
                return carry

            lax.fori_loop(0, bx, one, 0)

        def adjoint(n):
            gf = STEPS + n

            def one(x, carry):
                cent, shifted = centres(n, x)
                gc = [fld[gf, c, x + 2, pl.ds(Y0, 8), :] for c in range(3)]
                acc = [jnp.zeros((8, nz), jnp.float32)] * 3
                bcc = [jnp.zeros((8, nz), jnp.float32)] * 3
                m = jnp.zeros((8, nz), jnp.float32)
                for k, rev, off in bond_list():
                    w = vectors(n, x, off, cent, shifted)
                    g = [gc[c] - get(gf, c, x, off, gc[c]) for c in range(3)]
                    dot = w[0] * g[0] + w[1] * g[1] + w[2] * g[2]
                    kk = coef(k, rev, x)
                    t = kk * stretch(w, off) if n == STEPS - 1 else tval[n, 2 * k + rev, x]
                    r = kk * dot
                    if n and not rev:
                        m = m + t * dot
                    acc = [acc[c] + t * g[c] for c in range(3)]
                    bcc = [bcc[c] + r * w[c] for c in range(3)]
                for c in range(3):
                    a = anow[c, x] - TIME_STEP * (acc[c] + 2.0 * bcc[c])
                    if n:
                        anow[c, x] = a
                        fld[gf - 1, c, x + 2, pl.ds(Y0, 8), :] = gc[c] + TIME_STEP * a
                    else:
                        out_a[c, x] = a
                        out_g[c, x] = gc[c]
                if n:
                    msum[x] = m if n == STEPS - 1 else msum[x] + m
                return carry

            lax.fori_loop(0, bx, one, 0)

        for n in range(STEPS - 1):
            forward(n)
            send_field(n + 1)
            roll_own(n + 1)
            if n == 0:
                recv_field(2 * STEPS - 1)
            recv_field(n + 1)
        for n in range(STEPS - 1, 0, -1):
            adjoint(n)
            send_field(STEPS + n - 1)
            roll_own(STEPS + n - 1)
            recv_field(STEPS + n - 1)
        micro_part()

        lane = lax.broadcasted_iota(jnp.int32, (1, nz), 1)
        row = jnp.zeros((1, nz), jnp.float32)
        for cl in range(NCLASS):
            tot = jnp.zeros((8, nz), jnp.float32)
            for x in range(bx):
                tot = tot + jnp.where(material[x] == cl, msum[x], 0.0)
            one = jnp.sum(jnp.sum(tot, axis=0, keepdims=True), axis=1, keepdims=True)
            row = jnp.where(lane == cl, one * (TIME_STEP * inv_nodes) / micro[cl], row)
        mine[0] = row
        part[me] = row

        def share(j):
            return pltpu.make_async_remote_copy(
                src_ref=mine.at[0], dst_ref=part.at[me], send_sem=psem.at[j - 1], recv_sem=qsem.at[j - 1],
                device_id=peer(j), device_id_type=MESH,
            )

        def give(j, carry):
            share(j).start()
            return carry

        def take(j, carry):
            share(j).wait_recv()
            return carry

        def gone(j, carry):
            share(j).wait_send()
            return carry

        lax.fori_loop(1, nx * ny, give, 0)
        adjoint(0)
        lax.fori_loop(1, nx * ny, take, 0)
        tot = part[0]
        for j in range(1, nx * ny):
            tot = tot + part[j]
        out_m[...] = tot

        lax.fori_loop(1, nx * ny, gone, 0)
        for f in range(nf):
            for d in range(8):
                @pl.when(there(*DIRS[d]))
                def _():
                    copies(f, d).wait_send()
        for j, (sx, sy) in enumerate(KDIRS):
            @pl.when(there(sx, sy))
            def _():
                kcopy(j).wait_send()

    return kernel


def solution(mesh):
    nx, ny = mesh.shape["gx"], mesh.shape["gy"]

    def body(displacement, velocity, cuts, material, micromodulus, cot_disp, cot_vel):
        bx, by, nz = material.shape
        nf = 2 * STEPS
        f32 = jnp.float32
        vmem = pl.BlockSpec(memory_space=pltpu.VMEM)
        smem = pl.BlockSpec(memory_space=pltpu.SMEM)
        hbm = pl.BlockSpec(memory_space=pltpu.HBM)
        grad_a, grad_g, micro = pl.pallas_call(
            make_kernel(nx, ny, bx, by, nz),
            out_shape=(
                jax.ShapeDtypeStruct((3, bx, by, nz), f32),
                jax.ShapeDtypeStruct((3, bx, by, nz), f32),
                jax.ShapeDtypeStruct((1, nz), f32),
            ),
            in_specs=[hbm] * 4 + [smem] + [hbm] * 2,
            out_specs=(vmem, vmem, vmem),
            scratch_shapes=[
                pltpu.VMEM((nf, 3, bx + 4, 24, nz), f32),
                pltpu.VMEM((nf, 2, 3, bx + 4, 24, nz), f32),
                pltpu.VMEM((16, bx, 8, nz), jnp.int32),
                pltpu.VMEM((bx, 8, nz), jnp.int32),
                pltpu.VMEM((3, bx, 8, nz), f32),
                pltpu.VMEM((STEPS - 1, 32, bx, 8, nz), f32),
                pltpu.VMEM((16, bx + 4, 24, nz), f32),
                pltpu.VMEM((16, bx, 8, nz), f32),
                pltpu.VMEM((3, bx, 8, nz), f32),
                pltpu.VMEM((3, bx, 8, nz), f32),
                pltpu.VMEM((bx, 8, nz), f32),
                pltpu.VMEM((nf, 2, 6 * bx, nz), f32),
                pltpu.VMEM((nf, 2, 6 * bx, nz), f32),
                pltpu.VMEM((2, 6 * bx, nz), f32),
                pltpu.VMEM((nf, 4, 16, nz), f32),
                pltpu.VMEM((nf, 4, 16, nz), f32),
                pltpu.VMEM((8 * bx, nz), f32),
                pltpu.VMEM((8 * bx, nz), f32),
                pltpu.VMEM((3 * bx, nz), f32),
                pltpu.VMEM((3 * bx, nz), f32),
                pltpu.VMEM((2, 8, nz), f32),
                pltpu.VMEM((2, 8, nz), f32),
                pltpu.VMEM((nx * ny, 1, nz), f32),
                pltpu.VMEM((1, 1, nz), f32),
                pltpu.SemaphoreType.DMA((6,)),
                pltpu.SemaphoreType.DMA((nf, 8)),
                pltpu.SemaphoreType.DMA((nf, 8)),
                pltpu.SemaphoreType.DMA((6,)),
                pltpu.SemaphoreType.DMA((6,)),
                pltpu.SemaphoreType.DMA((nx * ny,)),
                pltpu.SemaphoreType.DMA((nx * ny,)),
            ],
            compiler_params=pltpu.CompilerParams(
                collective_id=0, has_side_effects=True, vmem_limit_bytes=40 * 1024 * 1024
            ),
        )(displacement, velocity, cuts, material, micromodulus, cot_disp, cot_vel)
        return grad_a, grad_g, micro[0, :NCLASS]

    return jax.shard_map(
        body,
        mesh=mesh,
        in_specs=(
            P(None, "gx", "gy", None),
            P(None, "gx", "gy", None),
            P(None, "gx", "gy", None),
            P("gx", "gy", None),
            P(),
            P(None, "gx", "gy", None),
            P(None, "gx", "gy", None),
        ),
        out_specs=(P(None, "gx", "gy", None), P(None, "gx", "gy", None), P()),
        check_vma=False,
    )
```

```python
import math

import jax
import jax.numpy as jnp
from jax import lax
from jax.experimental import pallas as pl
from jax.experimental.pallas import tpu as pltpu
from jax.sharding import PartitionSpec as P

STEPS = 4
NCLASS = 8
TIME_STEP = 0.2
MESH = pl.DeviceIdType.MESH

BONDS = (
    (0, 0, 1),
    (0, 0, 2),
    (0, 1, 0),
    (0, 1, 1),
    (0, 1, -1),
    (0, 2, 0),
    (1, 1, 0),
    (1, 1, 1),
    (1, 1, -1),
    (1, 0, 0),
    (1, 0, 1),
    (1, 0, -1),
    (1, -1, 0),
    (1, -1, 1),
    (1, -1, -1),
    (2, 0, 0),
)
REF_BONDS = (
    (1, 0, 0),
    (0, 1, 0),
    (0, 0, 1),
    (1, 1, 0),
    (1, -1, 0),
    (1, 0, 1),
    (1, 0, -1),
    (0, 1, 1),
    (0, 1, -1),
    (2, 0, 0),
    (0, 2, 0),
    (0, 0, 2),
    (1, 1, 1),
    (1, -1, 1),
    (1, 1, -1),
    (1, -1, -1),
)
CUT_ROW = tuple(REF_BONDS.index(o) for o in BONDS)
UP_Y = range(2, 9)
DOWN_Y = range(12, 15)
DIRS = ((1, 0), (-1, 0), (0, 1), (0, -1), (1, 1), (1, -1), (-1, 1), (-1, -1))
Y0 = 8


def make_kernel(nx, ny, bx, by, nz):
    assert by == 8 and nz == 128 and bx % 4 == 0 and bx >= 8
    nf = 2 * STEPS
    inv_nodes = 1.0 / math.sqrt(nx * bx * ny * by * nz)

    def kernel(
        disp, vel, cuts_in, material_in, micro, cot_d, cot_v,
        out_a, out_g, out_m,
        fld, rolled, cuts, material, cot_in, tval, stiff, back, vnow, anow, msum,
        pack_y, land_y, roll_y, pack_c, land_c,
        kpack_u, kland_u, kpack_d, kland_d, kpack_c, kland_c,
        part, mine,
        isem, ssem, rsem, kssem, krsem, psem, qsem,
    ):
        ix = lax.axis_index("gx")
        iy = lax.axis_index("gy")

        def there(sx, sy):
            ok = None
            for pos, step, count in ((ix, sx, nx), (iy, sy, ny)):
                if step:
                    one = (pos + step >= 0) & (pos + step < count)
                    ok = one if ok is None else ok & one
            return ok

        def who(sx, sy):
            return (ix + sx, iy + sy)

        barrier = pltpu.get_barrier_semaphore()
        me = ix * ny + iy

        def peer(j):
            to = lax.rem(me + j, nx * ny)
            return (to // ny, lax.rem(to, ny))

        def greet(j, carry):
            pl.semaphore_signal(barrier, inc=1, device_id=peer(j), device_id_type=MESH)
            return carry

        lax.fori_loop(1, nx * ny, greet, 0)

        loads = [
            pltpu.make_async_copy(src, dst, isem.at[j])
            for j, (src, dst) in enumerate((
                (cuts_in, cuts),
                (material_in, material),
                (disp, fld.at[0, :, pl.ds(2, bx), pl.ds(Y0, 8), :]),
                (cot_v, cot_in),
                (cot_d, anow),
                (vel, vnow),
            ))
        ]
        for cp in loads:
            cp.start()

        def copies(f, d):
            sx, sy = DIRS[d]
            if sy == 0:
                a, b = (bx, 0) if sx > 0 else (2, bx + 2)
                src = fld.at[f, :, pl.ds(a, 2), pl.ds(Y0, 8), :]
                dst = fld.at[f, :, pl.ds(b, 2), pl.ds(Y0, 8), :]
            elif sx == 0:
                e = 0 if sy > 0 else 1
                src, dst = pack_y.at[f, e], land_y.at[f, e]
            else:
                src, dst = pack_c.at[f, d - 4], land_c.at[f, d - 4]
            return pltpu.make_async_remote_copy(
                src_ref=src, dst_ref=dst, send_sem=ssem.at[f, d], recv_sem=rsem.at[f, d],
                device_id=who(sx, sy), device_id_type=MESH,
            )

        def send_field(f):
            for d in (0, 1):
                @pl.when(there(*DIRS[d]))
                def _():
                    copies(f, d).start()
            for d in (4, 5, 6, 7):
                sx, sy = DIRS[d]
                x0 = bx if sx > 0 else 2
                y0 = Y0 + 6 if sy > 0 else Y0
                @pl.when(there(sx, sy))
                def _():
                    for c in range(3):
                        for i in range(2):
                            pack_c[f, d - 4, pl.ds(c * 4 + i * 2, 2), :] = fld[f, c, x0 + i, pl.ds(y0, 2), :]
                    copies(f, d).start()
            for d in (2, 3):
                sx, sy = DIRS[d]
                y0 = Y0 + 6 if sy > 0 else Y0
                @pl.when(there(sx, sy))
                def _():
                    for c in range(3):
                        for i in range(bx):
                            pack_y[f, d - 2, pl.ds((c * bx + i) * 2, 2), :] = fld[f, c, 2 + i, pl.ds(y0, 2), :]
                    copies(f, d).start()

        def turn(val, dz):
            return pltpu.roll(val, (-dz) % nz, 1)

        def roll_own(f):
            def some(i, carry):
                for c in range(3):
                    for x in range(4):
                        val = fld[f, c, 2 + i * 4 + x, pl.ds(Y0, 8), :]
                        rolled[f, 0, c, 2 + i * 4 + x, pl.ds(Y0, 8), :] = turn(val, 1)
                        rolled[f, 1, c, 2 + i * 4 + x, pl.ds(Y0, 8), :] = turn(val, -1)
                return carry
            lax.fori_loop(0, bx // 4, some, 0)

        def recv_field(f, dirs=range(8)):
            for d in dirs:
                sx, sy = DIRS[d]
                y0 = Y0 - 2 if sy > 0 else Y0 + 8
                near = Y0 - 1 if sy > 0 else Y0 + 8
                j0 = 1 if sy > 0 else 0
                @pl.when(there(-sx, -sy))
                def _():
                    copies(f, d).wait_recv()
                    if sy == 0:
                        x = 1 if sx > 0 else bx + 2
                        for c in range(3):
                            val = fld[f, c, x, pl.ds(Y0, 8), :]
                            rolled[f, 0, c, x, pl.ds(Y0, 8), :] = turn(val, 1)
                            rolled[f, 1, c, x, pl.ds(Y0, 8), :] = turn(val, -1)
                    elif sx == 0:
                        for i in range(6 * bx // 8):
                            val = land_y[f, d - 2, pl.ds(i * 8, 8), :]
                            roll_y[0, pl.ds(i * 8, 8), :] = turn(val, 1)
                            roll_y[1, pl.ds(i * 8, 8), :] = turn(val, -1)
                        for c in range(3):
                            for i in range(bx):
                                r = (c * bx + i) * 2
                                fld[f, c, 2 + i, pl.ds(y0, 2), :] = land_y[f, d - 2, pl.ds(r, 2), :]
                                for z in range(2):
                                    rolled[f, z, c, 2 + i, pl.ds(near, 1), :] = roll_y[z, pl.ds(r + j0, 1), :]
                    else:
                        x = 1 if sx > 0 else bx + 2
                        i = 1 if sx > 0 else 0
                        for h in range(2):
                            val = land_c[f, d - 4, pl.ds(h * 8, 8), :]
                            roll_y[0, pl.ds(h * 8, 8), :] = turn(val, 1)
                            roll_y[1, pl.ds(h * 8, 8), :] = turn(val, -1)
                        for c in range(3):
                            r = c * 4 + i * 2 + j0
                            fld[f, c, x, pl.ds(near, 1), :] = land_c[f, d - 4, pl.ds(r, 1), :]
                            for z in range(2):
                                rolled[f, z, c, x, pl.ds(near, 1), :] = roll_y[z, pl.ds(r, 1), :]

        zero = jnp.zeros((8, nz), jnp.float32)
        zero24 = jnp.zeros((24, nz), jnp.float32)

        py = lax.broadcasted_iota(jnp.int32, (8, nz), 0) + iy * by
        pz = lax.broadcasted_iota(jnp.int32, (8, nz), 1)

        def own_stiff(x, carry):
            mat = material[x]
            mu = jnp.zeros((8, nz), jnp.float32)
            for cl in range(NCLASS):
                mu = jnp.where(mat == cl, micro[cl], mu)
            px = jnp.full((8, nz), ix * bx + x, jnp.int32)
            for k, (dx, dy, dz) in enumerate(BONDS):
                ok = None
                for pos, step, total in ((px, dx, nx * bx), (py, dy, ny * by), (pz, dz, nz)):
                    if step:
                        one = pos < total - step if step > 0 else pos >= -step
                        ok = one if ok is None else ok & one
                n2 = dx * dx + dy * dy + dz * dz
                scaled = mu * (0.5 / (n2 * math.sqrt(n2)))
                keep = scaled / (1.0 + cuts[CUT_ROW[k], x].astype(jnp.float32))
                stiff[k, 2 + x, pl.ds(Y0, 8), :] = jnp.where(ok, keep, 0.0)
            return carry

        loads[0].wait()
        loads[1].wait()
        lax.fori_loop(0, bx, own_stiff, 0)

        for cp in loads[2:]:
            cp.wait()
        for c in range(3):
            for x in range(bx):
                fld[2 * STEPS - 1, c, 2 + x, pl.ds(Y0, 8), :] = cot_in[c, x] + TIME_STEP * anow[c, x]

        pl.semaphore_wait(barrier, nx * ny - 1)
        send_field(0)

        def kcopies():
            return (
                (1, 0, stiff.at[pl.ds(6, 9), bx + 1, pl.ds(Y0, 8), :], stiff.at[pl.ds(6, 9), 1, pl.ds(Y0, 8), :]),
                (1, 0, stiff.at[15, pl.ds(bx, 2), pl.ds(Y0, 8), :], stiff.at[15, pl.ds(0, 2), pl.ds(Y0, 8), :]),
                (1, 1, kpack_c.at[0], kland_c.at[0]),
                (1, -1, kpack_c.at[1], kland_c.at[1]),
                (0, -1, kpack_d, kland_d),
                (0, 1, kpack_u, kland_u),
            )

        def kcopy(j):
            sx, sy, src, dst = kcopies()[j]
            return pltpu.make_async_remote_copy(
                src_ref=src, dst_ref=dst, send_sem=kssem.at[j], recv_sem=krsem.at[j],
                device_id=who(sx, sy), device_id_type=MESH,
            )

        KDIRS = ((1, 0), (1, 0), (1, 1), (1, -1), (0, -1), (0, 1))
        for j, (sx, sy) in enumerate(KDIRS):
            @pl.when(there(sx, sy))
            def _():
                row = Y0 + 7 if sy > 0 else Y0
                if j == 2 or j == 3:
                    for n, k in enumerate((6, 7, 8) if j == 2 else (12, 13, 14)):
                        kpack_c[j - 2, pl.ds(n, 1), :] = stiff[k, bx + 1, pl.ds(row, 1), :]
                if j == 4:
                    for n, k in enumerate(DOWN_Y):
                        for x in range(bx):
                            kpack_d[pl.ds(n * bx + x, 1), :] = stiff[k, 2 + x, pl.ds(row, 1), :]
                if j == 5:
                    for n, k in enumerate(UP_Y):
                        for x in range(bx):
                            kpack_u[pl.ds(n * bx + x, 1), :] = stiff[k, 2 + x, pl.ds(row, 1), :]
                    for x in range(bx):
                        kpack_u[pl.ds(7 * bx + x, 1), :] = stiff[5, 2 + x, pl.ds(row - 1, 1), :]
                kcopy(j).start()

        send_field(2 * STEPS - 1)
        roll_own(0)
        roll_own(2 * STEPS - 1)

        for cond, planes in ((ix == 0, (0, 1)), (ix == nx - 1, (bx + 2, bx + 3))):
            @pl.when(cond)
            def _():
                for f in range(nf):
                    for c in range(3):
                        for x in planes:
                            fld[f, c, x] = zero24
                        rolled[f, 0, c, planes[0] if planes[0] else 1] = zero24
                        rolled[f, 1, c, planes[0] if planes[0] else 1] = zero24
                if planes[0] == 0:
                    for k in range(6, 16):
                        for x in planes:
                            stiff[k, x] = zero24
        for cond, row in ((iy == 0, 0), (iy == ny - 1, 16)):
            @pl.when(cond)
            def _():
                def clear(x, carry):
                    for f in range(nf):
                        for c in range(3):
                            fld[f, c, x, pl.ds(row, 8), :] = zero
                            rolled[f, 0, c, x, pl.ds(row, 8), :] = zero
                            rolled[f, 1, c, x, pl.ds(row, 8), :] = zero
                    for k in UP_Y if row == 0 else DOWN_Y:
                        stiff[k, x, pl.ds(row, 8), :] = zero
                    return carry
                lax.fori_loop(0, bx + 4, clear, 0)

        recv_field(0)

        for j, (sx, sy) in enumerate(KDIRS):
            @pl.when(there(-sx, -sy))
            def _():
                kcopy(j).wait_recv()
                row = Y0 - 1 if sy > 0 else Y0 + 8
                if j == 2 or j == 3:
                    for n, k in enumerate((6, 7, 8) if j == 2 else (12, 13, 14)):
                        stiff[k, 1, pl.ds(row, 1), :] = kland_c[j - 2, pl.ds(n, 1), :]
                if j == 4:
                    for n, k in enumerate(DOWN_Y):
                        for x in range(bx):
                            stiff[k, 2 + x, pl.ds(row, 1), :] = kland_d[pl.ds(n * bx + x, 1), :]
                if j == 5:
                    for n, k in enumerate(UP_Y):
                        for x in range(bx):
                            stiff[k, 2 + x, pl.ds(row, 1), :] = kland_u[pl.ds(n * bx + x, 1), :]
                    for x in range(bx):
                        stiff[5, 2 + x, pl.ds(row - 1, 1), :] = kland_u[pl.ds(7 * bx + x, 1), :]

        def back_stiff(x, carry):
            for k, (dx, dy, dz) in enumerate(BONDS):
                val = stiff[k, 2 + x - dx, pl.ds(Y0 - dy, 8), :]
                if dz:
                    val = pltpu.roll(val, dz % nz, 1)
                back[k, x] = val
            return carry

        lax.fori_loop(0, bx, back_stiff, 0)

        def get(f, c, x, off, centre):
            dx, dy, dz = off
            if abs(dz) == 2:
                return turn(centre, dz)
            if dz:
                return rolled[f, 0 if dz > 0 else 1, c, x + 2 + dx, pl.ds(Y0 + dy, 8), :]
            return fld[f, c, x + 2 + dx, pl.ds(Y0 + dy, 8), :]

        def bond_list():
            for k, o in enumerate(BONDS):
                yield k, False, o
                yield k, True, tuple(-e for e in o)

        def coef(k, rev, x):
            return back[k, x] if rev else stiff[k, x + 2, pl.ds(Y0, 8), :]

        def vectors(f, x, off, cent, shifted):
            return [get(f, c, x, off, cent[c]) - shifted[c][off[c]] for c in range(3)]

        def centres(f, x):
            cent = [fld[f, c, x + 2, pl.ds(Y0, 8), :] for c in range(3)]
            shifted = [{e: cent[c] - float(e) for e in (-2, -1, 0, 1, 2)} for c in range(3)]
            return cent, shifted

        def stretch(w, off):
            return (w[0] * w[0] + w[1] * w[1] + w[2] * w[2]) - float(sum(e * e for e in off))

        ALONG_Y = (2, 3)
        OTHERS = (0, 1, 4, 5, 6, 7)

        def sweep(one, late):
            def edge(i, carry):
                return one(i + (i // 2) * (bx - 4), carry)

            lax.fori_loop(2, bx - 2, one, 0)
            if late is not None:
                recv_field(late, OTHERS)
            lax.fori_loop(0, 4, edge, 0)

        def forward(n, late):
            def one(x, carry):
                cent, shifted = centres(n, x)
                acc = [jnp.zeros((8, nz), jnp.float32)] * 3
                for k, rev, off in bond_list():
                    w = vectors(n, x, off, cent, shifted)
                    t = coef(k, rev, x) * stretch(w, off)
                    tval[n, 2 * k + rev, x] = t
                    acc = [acc[c] + t * w[c] for c in range(3)]
                for c in range(3):
                    v = vnow[c, x] + TIME_STEP * acc[c]
                    vnow[c, x] = v
                    fld[n + 1, c, x + 2, pl.ds(Y0, 8), :] = cent[c] + TIME_STEP * v
                return carry

            sweep(one, late)

        def micro_part(late):
            def one(x, carry):
                cent, shifted = centres(0, x)
                gc = [fld[STEPS, c, x + 2, pl.ds(Y0, 8), :] for c in range(3)]
                m = msum[x]
                for k, rev, off in bond_list():
                    if rev:
                        continue
                    w = vectors(0, x, off, cent, shifted)
                    g = [gc[c] - get(STEPS, c, x, off, gc[c]) for c in range(3)]
                    m = m + tval[0, 2 * k, x] * (w[0] * g[0] + w[1] * g[1] + w[2] * g[2])
                msum[x] = m
                return carry

            sweep(one, late)

        def adjoint(n, late):
            gf = STEPS + n

            def one(x, carry):
                cent, shifted = centres(n, x)
                gc = [fld[gf, c, x + 2, pl.ds(Y0, 8), :] for c in range(3)]
                acc = [jnp.zeros((8, nz), jnp.float32)] * 3
                bcc = [jnp.zeros((8, nz), jnp.float32)] * 3
                m = jnp.zeros((8, nz), jnp.float32)
                for k, rev, off in bond_list():
                    w = vectors(n, x, off, cent, shifted)
                    g = [gc[c] - get(gf, c, x, off, gc[c]) for c in range(3)]
                    dot = w[0] * g[0] + w[1] * g[1] + w[2] * g[2]
                    kk = coef(k, rev, x)
                    t = kk * stretch(w, off) if n == STEPS - 1 else tval[n, 2 * k + rev, x]
                    r = kk * dot
                    if n and not rev:
                        m = m + t * dot
                    acc = [acc[c] + t * g[c] for c in range(3)]
                    bcc = [bcc[c] + r * w[c] for c in range(3)]
                for c in range(3):
                    a = anow[c, x] - TIME_STEP * (acc[c] + 2.0 * bcc[c])
                    anow[c, x] = a
                    if n:
                        fld[gf - 1, c, x + 2, pl.ds(Y0, 8), :] = gc[c] + TIME_STEP * a
                if n:
                    msum[x] = m if n == STEPS - 1 else msum[x] + m
                return carry

            sweep(one, late)

        for n in range(STEPS - 1):
            forward(n, n if n else None)
            send_field(n + 1)
            roll_own(n + 1)
            if n == 0:
                recv_field(2 * STEPS - 1)
            recv_field(n + 1, ALONG_Y)
        for n in range(STEPS - 1, 0, -1):
            adjoint(n, n if n == STEPS - 1 else STEPS + n)
            send_field(STEPS + n - 1)
            roll_own(STEPS + n - 1)
            recv_field(STEPS + n - 1, ALONG_Y)
        store_g = pltpu.make_async_copy(fld.at[STEPS, :, pl.ds(2, bx), pl.ds(Y0, 8), :], out_g, isem.at[0])
        store_g.start()
        micro_part(STEPS)

        lane = lax.broadcasted_iota(jnp.int32, (1, nz), 1)
        row = jnp.zeros((1, nz), jnp.float32)
        for cl in range(NCLASS):
            tot = jnp.zeros((8, nz), jnp.float32)
            for x in range(bx):
                tot = tot + jnp.where(material[x] == cl, msum[x], 0.0)
            one = jnp.sum(jnp.sum(tot, axis=0, keepdims=True), axis=1, keepdims=True)
            row = jnp.where(lane == cl, one * (TIME_STEP * inv_nodes) / micro[cl], row)
        mine[0] = row
        part[me] = row

        def share(j):
            return pltpu.make_async_remote_copy(
                src_ref=mine.at[0], dst_ref=part.at[me], send_sem=psem.at[j - 1], recv_sem=qsem.at[j - 1],
                device_id=peer(j), device_id_type=MESH,
            )

        def give(j, carry):
            share(j).start()
            return carry

        def take(j, carry):
            share(j).wait_recv()
            return carry

        def gone(j, carry):
            share(j).wait_send()
            return carry

        lax.fori_loop(1, nx * ny, give, 0)
        adjoint(0, None)
        store_a = pltpu.make_async_copy(anow, out_a, isem.at[1])
        store_a.start()
        lax.fori_loop(1, nx * ny, take, 0)
        tot = part[0]
        for j in range(1, nx * ny):
            tot = tot + part[j]
        out_m[...] = tot
        store_g.wait()
        store_a.wait()

        lax.fori_loop(1, nx * ny, gone, 0)
        for f in range(nf):
            for d in range(8):
                @pl.when(there(*DIRS[d]))
                def _():
                    copies(f, d).wait_send()
        for j, (sx, sy) in enumerate(KDIRS):
            @pl.when(there(sx, sy))
            def _():
                kcopy(j).wait_send()

    return kernel


def solution(mesh):
    nx, ny = mesh.shape["gx"], mesh.shape["gy"]

    def body(displacement, velocity, cuts, material, micromodulus, cot_disp, cot_vel):
        bx, by, nz = material.shape
        nf = 2 * STEPS
        f32 = jnp.float32
        vmem = pl.BlockSpec(memory_space=pltpu.VMEM)
        smem = pl.BlockSpec(memory_space=pltpu.SMEM)
        hbm = pl.BlockSpec(memory_space=pltpu.HBM)
        grad_a, grad_g, micro = pl.pallas_call(
            make_kernel(nx, ny, bx, by, nz),
            out_shape=(
                jax.ShapeDtypeStruct((3, bx, by, nz), f32),
                jax.ShapeDtypeStruct((3, bx, by, nz), f32),
                jax.ShapeDtypeStruct((1, nz), f32),
            ),
            in_specs=[hbm] * 4 + [smem] + [hbm] * 2,
            out_specs=(hbm, hbm, vmem),
            scratch_shapes=[
                pltpu.VMEM((nf, 3, bx + 4, 24, nz), f32),
                pltpu.VMEM((nf, 2, 3, bx + 4, 24, nz), f32),
                pltpu.VMEM((16, bx, 8, nz), jnp.int32),
                pltpu.VMEM((bx, 8, nz), jnp.int32),
                pltpu.VMEM((3, bx, 8, nz), f32),
                pltpu.VMEM((STEPS - 1, 32, bx, 8, nz), f32),
                pltpu.VMEM((16, bx + 4, 24, nz), f32),
                pltpu.VMEM((16, bx, 8, nz), f32),
                pltpu.VMEM((3, bx, 8, nz), f32),
                pltpu.VMEM((3, bx, 8, nz), f32),
                pltpu.VMEM((bx, 8, nz), f32),
                pltpu.VMEM((nf, 2, 6 * bx, nz), f32),
                pltpu.VMEM((nf, 2, 6 * bx, nz), f32),
                pltpu.VMEM((2, 6 * bx, nz), f32),
                pltpu.VMEM((nf, 4, 16, nz), f32),
                pltpu.VMEM((nf, 4, 16, nz), f32),
                pltpu.VMEM((8 * bx, nz), f32),
                pltpu.VMEM((8 * bx, nz), f32),
                pltpu.VMEM((3 * bx, nz), f32),
                pltpu.VMEM((3 * bx, nz), f32),
                pltpu.VMEM((2, 8, nz), f32),
                pltpu.VMEM((2, 8, nz), f32),
                pltpu.VMEM((nx * ny, 1, nz), f32),
                pltpu.VMEM((1, 1, nz), f32),
                pltpu.SemaphoreType.DMA((6,)),
                pltpu.SemaphoreType.DMA((nf, 8)),
                pltpu.SemaphoreType.DMA((nf, 8)),
                pltpu.SemaphoreType.DMA((6,)),
                pltpu.SemaphoreType.DMA((6,)),
                pltpu.SemaphoreType.DMA((nx * ny,)),
                pltpu.SemaphoreType.DMA((nx * ny,)),
            ],
            compiler_params=pltpu.CompilerParams(
                collective_id=0, has_side_effects=True, vmem_limit_bytes=63 * 1024 * 1024 + 768 * 1024
            ),
        )(displacement, velocity, cuts, material, micromodulus, cot_disp, cot_vel)
        return grad_a, grad_g, micro[0, :NCLASS]

    return jax.shard_map(
        body,
        mesh=mesh,
        in_specs=(
            P(None, "gx", "gy", None),
            P(None, "gx", "gy", None),
            P(None, "gx", "gy", None),
            P("gx", "gy", None),
            P(),
            P(None, "gx", "gy", None),
            P(None, "gx", "gy", None),
        ),
        out_specs=(P(None, "gx", "gy", None), P(None, "gx", "gy", None), P()),
        check_vma=False,
    )
```
